512 devices in a mesh: ev: 16 (over z), asset: 32 (over x, y, core).
Axes of the slice: x: 4, y: 4, z: 16, core: 2. Of those that a mesh axis runs over, the one named last changes fastest.
Arguments:
- hazard: bfloat16 [512, 163840], P('ev', 'asset'), may hold values from 0 to 1
- route_tiles: int32 [32, 64], P('asset'), may hold values from 0 to 4
- block_slots: int32 [4, 512], P(None, 'asset'), may hold values from 0 to 63, as said below
- corner_cells: int32 [4, 131072], P(None, 'asset'), may hold values from 0 to 4095
- corner_weights: float32 [4, 131072], P(None, 'asset'), may hold values from 0.05 to 1
- block_class: int32 [512], P('asset'), may hold values from 0 to 15
- curves: float32 [16, 16], replicated, may hold values from 0 to 1
- exposure: float32 [3, 131072], P(None, 'asset'), may hold values from 0.1 to 10
- event_ssp: int32 [512], P('ev'), may hold values from 0 to 2
- operator: bfloat16 [128, 131072], P('ev', 'asset'), may hold values from -0.03125 to 0.03125
Outputs:
- benefit: float32 [512, 128], P(('ev', 'asset'))
The draws below stay inside these ranges and needn't reach their ends.
Inputs may be any that keep to these rules, and one draw needn't show every extreme that they name: `block_slots`: the 16 blocks of each device name each of its 64 slots.
All inputs are finite; a program needn't handle non-finite values.
Results may differ from the reference program's by a relative error of at most 0.0003.
Values may be sent and summed in bfloat16 or wider, within the bound.
No kernel may reach another device: no remote copies, remote signals or barrier semaphores. Data moves between devices by JAX's collectives and lax.ppermute only.
A program may use at most 64 MiB of HBM per device.

```python
import math
import jax
import jax.numpy as jnp
from jax import lax

AB_DEV = 16
HT_DEV = 5
CAP = 2
TILE = 1024
BLOCK = 256
OVL = 4
CORNERS = 4
SSPS = 3
CLASSES = 16
LEVELS = 16
MEASURE_COUNT = 128
ASSET_DEVS = 32
SLOTS = 64
EVENTS = 512
BLOCKS = 512
TOTAL_ASSETS = 131072
HTILES = 160


def draw_block_slots(key, part):
    key = jax.random.fold_in(key, 7)
    count = OVL * AB_DEV
    base = jnp.arange(count, dtype=jnp.int32) % SLOTS
    keys = jax.random.split(key, ASSET_DEVS)
    mixed = jax.vmap(lambda single: jax.random.permutation(single, base))(keys)
    return mixed.reshape(ASSET_DEVS, OVL, AB_DEV).transpose(1, 0, 2).reshape(OVL, BLOCKS)


def set_ends(array, rng, low, largest):
    longest = array.shape.index(max(array.shape))
    spots = []
    for shift in (0, 1):
        where = [jax.random.randint(jax.random.fold_in(rng, axis), (), 0, length) for axis, length in enumerate(array.shape)]
        where[longest] = (where[longest] + shift) % array.shape[longest]
        spots.append(tuple(where))
    return array.at[spots[0]].set(low).at[spots[1]].set(largest)


def spiked(values, rng, source, target, blocks, factor):
    def block_of(dim):
        return (jnp.arange(values.shape[dim]) // (values.shape[dim] // blocks)).reshape((-1,) + (1,) * (values.ndim - 1 - dim))

    first = jax.random.permutation(rng, blocks)[block_of(target)]
    far = (block_of(target) + blocks // 2) % blocks
    return jnp.where((block_of(source) == first) | (block_of(source) == far), factor * values, values)


def levels(stream_key, shape, pieces, low, high):
    factor_of, own = 1.0, jax.random.fold_in(stream_key, 6)
    for axis_at, shards_of in pieces:
        steps = jnp.exp(jax.random.uniform(jax.random.fold_in(own, axis_at), (shards_of,), jnp.float32, low / len(pieces), high / len(pieces)))
        factor_of = factor_of * jnp.repeat(steps, shape[axis_at] // shards_of).reshape([-1 if axis == axis_at else 1 for axis in range(len(shape))])
    return factor_of


def bell_draw_with(rng, shape, deviation, bound, pieces, heavy, kind=jnp.bfloat16):
    values = deviation * jax.random.normal(rng, shape, jnp.float32)
    if pieces:
        values = values * levels(rng, shape, pieces, -0.22, 0.18)
    return jnp.clip(spiked(values, jax.random.fold_in(rng, 3), *heavy), -bound, bound).astype(kind)


def setup_inputs(seed: int = 0) -> dict:
    splits = jax.random.split(jax.random.key(seed), 11)
    return {
        "hazard": jnp.clip(1.0 * jax.random.uniform(splits[0], (EVENTS, HTILES * TILE), jnp.float32) ** levels(splits[0], (EVENTS, HTILES * TILE), ((0, 16), (1, 32)), -0.2, 0.2), 0.0, 1.0).astype(jnp.bfloat16),
        "route_tiles": set_ends(jax.random.randint(splits[1], (ASSET_DEVS, SLOTS), 0, HT_DEV), jax.random.fold_in(splits[1], 1), 0, HT_DEV - 1).astype(jnp.int32),
        "block_slots": draw_block_slots(jax.random.fold_in(splits[10], 71), 0),
        "corner_cells": set_ends(jax.random.randint(splits[3], (CORNERS, TOTAL_ASSETS), 0, OVL * TILE), jax.random.fold_in(splits[3], 1), 0, (OVL * TILE) - 1).astype(jnp.int32),
        "corner_weights": jnp.clip(0.05 + 0.95 * jax.random.uniform(splits[4], (CORNERS, TOTAL_ASSETS), jnp.float32) ** levels(splits[4], (CORNERS, TOTAL_ASSETS), ((1, 32),), -0.2, 0.2), 0.05, 1.0),
        "block_class": set_ends(jax.random.randint(splits[5], (BLOCKS,), 0, CLASSES), jax.random.fold_in(splits[5], 1), 0, CLASSES - 1).astype(jnp.int32),
        "curves": jnp.clip(jax.random.uniform(splits[6], (CLASSES, LEVELS), jnp.float32, 0.0, 1.0), 0.0, 1.0),
        "exposure": jnp.clip(jnp.exp(math.log(10.0) - 4.6051702 * jax.random.uniform(splits[7], (SSPS, TOTAL_ASSETS), jnp.float32) ** levels(splits[7], (SSPS, TOTAL_ASSETS), ((1, 32),), -0.2, 0.2)), 0.1, 10.0),
        "event_ssp": set_ends(jax.random.randint(splits[8], (EVENTS,), 0, SSPS), jax.random.fold_in(splits[8], 1), 0, SSPS - 1).astype(jnp.int32),
        "operator": bell_draw_with(splits[9], (MEASURE_COUNT, TOTAL_ASSETS), TOTAL_ASSETS ** -0.5, 0.03125, ((0, 16), (1, 32)), (1, 0, 32, 2.75)),
    }


def shard_benefit(device, hazard, route_tiles, block_slots, corner_cells, corner_weights, block_class, curves, exposure, event_ssp, operator):
    span = AB_DEV * BLOCK
    begin = (device * span).astype(jnp.int32)
    routes = lax.dynamic_slice_in_dim(route_tiles, (device * CAP).astype(jnp.int32), CAP, 1)
    tile_ids = (jnp.arange(ASSET_DEVS, dtype=jnp.int32)[:, None] * HT_DEV + routes).reshape(SLOTS)
    slots_here = lax.dynamic_slice_in_dim(block_slots, (device * AB_DEV).astype(jnp.int32), AB_DEV, 1)
    cells = lax.dynamic_slice_in_dim(corner_cells, begin, span, 1)
    weights = lax.dynamic_slice_in_dim(corner_weights, begin, span, 1)
    block_index = jnp.arange(span, dtype=jnp.int32) // BLOCK
    chosen = slots_here[cells // TILE, block_index[None, :]]
    columns = tile_ids[chosen] * TILE + cells % TILE
    values = hazard[:, columns.reshape(-1)].reshape(EVENTS, CORNERS, span)
    hazard_intensity = jnp.sum(weights[None] * values.astype(jnp.float32), axis=1) / jnp.sum(weights, axis=0)[None]
    classes = lax.dynamic_slice_in_dim(block_class, (device * AB_DEV).astype(jnp.int32), AB_DEV, 0)
    asset_curves = curves[classes][block_index]
    rescaled_values = (LEVELS - 1) * hazard_intensity
    ratio = jnp.zeros_like(hazard_intensity)
    for position in range(LEVELS):
        ratio = ratio + asset_curves[:, position][None] * jnp.maximum(0.0, 1.0 - jnp.abs(rescaled_values - position))
    values_here = lax.dynamic_slice_in_dim(exposure, begin, span, 1)
    impact = values_here[event_ssp] * ratio
    rows = lax.dynamic_slice_in_dim(operator, begin, span, 1).astype(jnp.float32)
    return lax.dot_general(impact, rows, (((1,), (1,)), ((), ())), precision=lax.Precision.HIGHEST)


def reference(hazard, route_tiles, block_slots, corner_cells, corner_weights, block_class, curves, exposure, event_ssp, operator):
    def single(device):
        return shard_benefit(device, hazard, route_tiles, block_slots, corner_cells, corner_weights, block_class, curves, exposure, event_ssp, operator)

    partial_sums = lax.map(single, jnp.arange(ASSET_DEVS, dtype=jnp.int32))
    return jnp.sum(partial_sums, axis=0)
```

```python
import functools
import jax
import jax.numpy as jnp
from jax import lax
from jax.experimental import pallas as pl
from jax.experimental.pallas import tpu as pltpu
from jax.sharding import PartitionSpec as P

TILE = 1024
BLOCK = 256
OVL = 4
CORNERS = 4
SSPS = 3
CLASSES = 16
LEVELS = 16
LANES = 128
SUB = 8
DEPTH = 256


def pack_kernel(route_ref, hazard_ref, out_ref, sems):
    def copy(slot):
        first = pl.multiple_of(route_ref[0, slot] * TILE, TILE)
        return pltpu.make_async_copy(hazard_ref.at[:, pl.ds(first, TILE)], out_ref.at[slot], sems.at[slot])

    @pl.loop(0, out_ref.shape[0])
    def _(slot):
        copy(slot).start()

    @pl.loop(0, out_ref.shape[0])
    def _(slot):
        copy(slot).wait()


def pick_kernel(
    slots_ref, class_ref, tiles_ref, cells_ref, weights_ref, curves_ref, exposure_ref, ssp_ref, out_ref, window_ref, sems
):
    events = out_ref.shape[0]
    blocks = slots_ref.shape[1]
    pieces = TILE // DEPTH
    groups = events // SUB
    rows = lax.broadcasted_iota(jnp.int32, (DEPTH, BLOCK), 0)

    def fetch(block, k):
        at = lax.rem(block, 2)
        return pltpu.make_async_copy(tiles_ref.at[slots_ref[k, block]], window_ref.at[at, k], sems.at[at, k])

    for k in range(OVL):
        fetch(0, k).start()

    @pl.loop(0, blocks)
    def _(block):
        @pl.when(block + 1 < blocks)
        def _():
            for k in range(OVL):
                fetch(block + 1, k).start()

        for k in range(OVL):
            fetch(block, k).wait()
        at = lax.rem(block, 2)
        assets = pl.ds(pl.multiple_of(block * BLOCK, BLOCK), BLOCK)
        window = [
            window_ref[at, k, :, piece * DEPTH : (piece + 1) * DEPTH] for k in range(OVL) for piece in range(pieces)
        ]
        window = jnp.concatenate(window, axis=0)
        weights = [jnp.broadcast_to(weights_ref[pl.ds(at, 1), assets], (SUB, BLOCK)) for at in range(CORNERS)]
        scale = (LEVELS - 1) / (weights[0] + weights[1] + weights[2] + weights[3])
        place = [jnp.zeros((SUB, BLOCK), jnp.float32)] * groups
        for corner in range(CORNERS):
            cell = cells_ref[pl.ds(corner, 1), assets]
            picker = jnp.where(rows == (cell & (DEPTH - 1)), 1.0, 0.0).astype(jnp.bfloat16)
            found = jnp.dot(window, picker, preferred_element_type=jnp.float32)
            high = jnp.broadcast_to(cell, (SUB, BLOCK)) // DEPTH
            value = [found[group * SUB : (group + 1) * SUB] for group in range(groups)]
            for part in range(1, OVL * pieces):
                here = high == part
                for group in range(groups):
                    first = part * events + group * SUB
                    value[group] = jnp.where(here, found[first : first + SUB], value[group])
            place = [place[group] + weights[corner] * value[group] for group in range(groups)]
        row = class_ref[block]
        curve = jnp.broadcast_to(curves_ref[pl.ds(row, 1), :], (SUB, LANES))
        values = [jnp.broadcast_to(exposure_ref[pl.ds(at, 1), assets], (SUB, BLOCK)) for at in range(SSPS)]
        for group in range(groups):
            lines = slice(group * SUB, (group + 1) * SUB)
            spot = place[group] * scale
            level = jnp.clip(spot.astype(jnp.int32), 0, LEVELS - 2)
            part = spot - level.astype(jnp.float32)
            base, top = [], []
            for half in range(BLOCK // LANES):
                here = level[:, half * LANES : (half + 1) * LANES]
                base.append(jnp.take_along_axis(curve, here, axis=1, mode="promise_in_bounds"))
                top.append(jnp.take_along_axis(curve, here + 1, axis=1, mode="promise_in_bounds"))
            base, top = jnp.concatenate(base, axis=1), jnp.concatenate(top, axis=1)
            scenario = jnp.concatenate([ssp_ref[lines, :]] * (BLOCK // LANES), axis=1)
            value = jnp.where(scenario == 0, values[0], jnp.where(scenario == 1, values[1], values[2]))
            out_ref[lines, assets] = value * (base * (1.0 - part) + top * part)


def product_kernel(impact_ref, near_ref, far_ref, order_ref, out_ref):
    step = 512
    events, half = impact_ref.shape[0], near_ref.shape[0]
    dims = (((1,), (1,)), ((), ()))
    total = jnp.zeros((events, 2 * half), jnp.float32)
    for first in range(0, impact_ref.shape[1], step):
        impact = impact_ref[:, first : first + step]
        rows = jnp.concatenate([near_ref[:, first : first + step], far_ref[:, first : first + step]], axis=0)
        top = impact.astype(jnp.bfloat16)
        rest = (impact - top.astype(jnp.float32)).astype(jnp.bfloat16)
        both = jnp.concatenate([top, rest], axis=0)
        sums = lax.dot_general(both, rows, dims, preferred_element_type=jnp.float32)
        total = total + (sums[:events] + sums[events:])
    order = jnp.broadcast_to(order_ref[...], total.shape)
    out_ref[...] = jnp.take_along_axis(total, order, axis=1, mode="promise_in_bounds")


def vmem():
    return pl.BlockSpec(memory_space=pltpu.VMEM)


def smem():
    return pl.BlockSpec(memory_space=pltpu.SMEM)


def params():
    return pltpu.CompilerParams(vmem_limit_bytes=40 * 1024 * 1024)


def cost(flops, moved):
    return pl.CostEstimate(flops=flops, bytes_accessed=moved, transcendentals=0)


def shards(
    hazard,
    route_tiles,
    block_slots,
    corner_cells,
    corner_weights,
    block_class,
    curves,
    exposure,
    event_ssp,
    operator,
):
    events = hazard.shape[0]
    devices = lax.axis_size("asset")
    layers = lax.axis_size("ev")
    slots = route_tiles.shape[1]
    span = corner_cells.shape[1]
    with jax.named_scope("measures"):
        near = operator
        hops = []
        hop = layers // 2
        while hop:
            far = lax.ppermute(near, "ev", [(i, i ^ hop) for i in range(layers)])
            hops.append(hop)
            hop //= 2
            if hop:
                near = jnp.concatenate([near, far], axis=0)
        measures = operator.shape[0]
        owner = jnp.arange(layers * measures, dtype=jnp.int32) // measures ^ lax.axis_index("ev")
        place = sum(jnp.where(owner & hop, 1 << at, 0) for at, hop in enumerate(hops))
        order = place * measures + jnp.arange(layers * measures, dtype=jnp.int32) % measures
    with jax.named_scope("pack"):
        packed = pl.pallas_call(
            pack_kernel,
            out_shape=jax.ShapeDtypeStruct((slots, events, TILE), jnp.bfloat16),
            in_specs=[smem(), vmem()],
            out_specs=pl.BlockSpec(memory_space=pltpu.HBM),
            scratch_shapes=[pltpu.SemaphoreType.DMA((slots,))],
            compiler_params=params(),
            cost_estimate=cost(0, 8 * slots * events * TILE),
        )(route_tiles, hazard)
    with jax.named_scope("tiles"):
        tiles = lax.all_to_all(packed.reshape(devices, -1, TILE), "asset", 0, 0)
        tiles = tiles.reshape(slots, events, TILE)
    wide = jnp.pad(curves, ((0, 0), (0, LANES - LEVELS)))
    ssp = jnp.broadcast_to(event_ssp[:, None], (events, LANES))
    with jax.named_scope("pick"):
        impact = pl.pallas_call(
            pick_kernel,
            out_shape=jax.ShapeDtypeStruct((events, span), jnp.float32),
            in_specs=[smem(), smem(), pl.BlockSpec(memory_space=pl.ANY)] + [vmem()] * 5,
            out_specs=vmem(),
            scratch_shapes=[
                pltpu.VMEM((2, OVL, events, TILE), jnp.bfloat16),
                pltpu.SemaphoreType.DMA((2, OVL)),
            ],
            compiler_params=params(),
            cost_estimate=cost(2 * CORNERS * OVL * TILE * events * span, 2 * slots * events * TILE),
        )(block_slots, block_class, tiles, corner_cells, corner_weights, wide, exposure, ssp)
    with jax.named_scope("product"):
        terms = pl.pallas_call(
            product_kernel,
            out_shape=jax.ShapeDtypeStruct((events, order.shape[0]), jnp.float32),
            in_specs=[vmem()] * 4,
            out_specs=vmem(),
            compiler_params=params(),
            cost_estimate=cost(4 * events * order.shape[0] * span, 2 * order.shape[0] * span),
        )(impact, near, far, order[None])
    with jax.named_scope("sums"):
        parts = lax.all_to_all(terms[:, None, :], "asset", 0, 0)
        return jnp.sum(parts, axis=0)


def solution(mesh):
    in_specs = (
        P("ev", "asset"),
        P("asset", None),
        P(None, "asset"),
        P(None, "asset"),
        P(None, "asset"),
        P("asset"),
        P(),
        P(None, "asset"),
        P("ev"),
        P("ev", "asset"),
    )
    out_specs = P(("ev", "asset"), None)
    return jax.shard_map(shards, mesh=mesh, in_specs=in_specs, out_specs=out_specs, check_vma=False)
```

```python
import functools
import jax
import jax.numpy as jnp
from jax import lax
from jax.experimental import pallas as pl
from jax.experimental.pallas import tpu as pltpu
from jax.sharding import PartitionSpec as P

TILE = 1024
BLOCK = 256
OVL = 4
CORNERS = 4
SSPS = 3
CLASSES = 16
LEVELS = 16
LANES = 128
SUB = 8
DEPTH = 256


def pack_kernel(routes_ref, tiles_ref, out_ref, route_ref, hazard_ref, first_sems, sems):
    route = pltpu.make_async_copy(routes_ref, route_ref, first_sems.at[0])
    hazard = pltpu.make_async_copy(tiles_ref, hazard_ref, first_sems.at[1])
    route.start()
    hazard.start()
    route.wait()
    hazard.wait()

    def copy(slot):
        first = pl.multiple_of(route_ref[0, slot] * TILE, TILE)
        return pltpu.make_async_copy(hazard_ref.at[:, pl.ds(first, TILE)], out_ref.at[slot], sems.at[slot])

    @pl.loop(0, out_ref.shape[0])
    def _(slot):
        copy(slot).start()

    @pl.loop(0, out_ref.shape[0])
    def _(slot):
        copy(slot).wait()


def pick_kernel(
    slots_ref, class_ref, tiles_ref, cells_ref, weights_ref, curves_ref, exposure_ref, ssp_ref, out_ref
):
    events = out_ref.shape[0]
    pieces = TILE // DEPTH
    groups = events // SUB
    rows = lax.broadcasted_iota(jnp.int32, (DEPTH, BLOCK), 0)

    @pl.loop(0, slots_ref.shape[1], unroll=4)
    def _(block):
        assets = pl.ds(pl.multiple_of(block * BLOCK, BLOCK), BLOCK)
        window = [
            tiles_ref[slots_ref[k, block], :, piece * DEPTH : (piece + 1) * DEPTH]
            for k in range(OVL)
            for piece in range(pieces)
        ]
        cells = [cells_ref[pl.ds(corner, 1), assets] for corner in range(CORNERS)]
        picker = [jnp.where(rows == (cell & (DEPTH - 1)), 1.0, 0.0).astype(jnp.bfloat16) for cell in cells]
        found = jnp.dot(
            jnp.concatenate(window, axis=0), jnp.concatenate(picker, axis=1), preferred_element_type=jnp.float32
        )
        weights = [jnp.broadcast_to(weights_ref[pl.ds(at, 1), assets], (SUB, BLOCK)) for at in range(CORNERS)]
        scale = (LEVELS - 1) / (weights[0] + weights[1] + weights[2] + weights[3])
        place = [jnp.zeros((SUB, BLOCK), jnp.float32)] * groups
        for corner in range(CORNERS):
            high = jnp.broadcast_to(cells[corner], (SUB, BLOCK)) // DEPTH
            mine = found[:, corner * BLOCK : (corner + 1) * BLOCK]
            value = [mine[group * SUB : (group + 1) * SUB] for group in range(groups)]
            for part in range(1, OVL * pieces):
                here = high == part
                for group in range(groups):
                    first = part * events + group * SUB
                    value[group] = jnp.where(here, mine[first : first + SUB], value[group])
            place = [place[group] + weights[corner] * value[group] for group in range(groups)]
        row = class_ref[block]
        curve = jnp.broadcast_to(curves_ref[pl.ds(row, 1), :], (SUB, LANES))
        values = [jnp.broadcast_to(exposure_ref[pl.ds(at, 1), assets], (SUB, BLOCK)) for at in range(SSPS)]
        for group in range(groups):
            lines = slice(group * SUB, (group + 1) * SUB)
            spot = place[group] * scale
            level = jnp.clip(spot.astype(jnp.int32), 0, LEVELS - 2)
            part = spot - level.astype(jnp.float32)
            base, top = [], []
            for half in range(BLOCK // LANES):
                here = level[:, half * LANES : (half + 1) * LANES]
                base.append(jnp.take_along_axis(curve, here, axis=1, mode="promise_in_bounds"))
                top.append(jnp.take_along_axis(curve, here + 1, axis=1, mode="promise_in_bounds"))
            base, top = jnp.concatenate(base, axis=1), jnp.concatenate(top, axis=1)
            scenario = jnp.concatenate([ssp_ref[lines, :]] * (BLOCK // LANES), axis=1)
            value = jnp.where(scenario == 0, values[0], jnp.where(scenario == 1, values[1], values[2]))
            out_ref[lines, assets] = value * (base * (1.0 - part) + top * part)


def product_kernel(impact_ref, order_ref, *refs):
    *rows_refs, out_ref = refs
    step = 512
    events = impact_ref.shape[0]
    dims = (((1,), (1,)), ((), ()))
    total = jnp.zeros(out_ref.shape, jnp.float32)
    for first in range(0, impact_ref.shape[1], step):
        impact = impact_ref[:, first : first + step]
        rows = jnp.concatenate([ref[:, first : first + step] for ref in rows_refs], axis=0)
        top = impact.astype(jnp.bfloat16)
        rest = (impact - top.astype(jnp.float32)).astype(jnp.bfloat16)
        both = jnp.concatenate([top, rest], axis=0)
        sums = lax.dot_general(both, rows, dims, preferred_element_type=jnp.float32)
        total = total + (sums[:events] + sums[events:])
    order = jnp.broadcast_to(order_ref[...], total.shape)
    out_ref[...] = jnp.take_along_axis(total, order, axis=1, mode="promise_in_bounds")


def vmem():
    return pl.BlockSpec(memory_space=pltpu.VMEM)


def smem():
    return pl.BlockSpec(memory_space=pltpu.SMEM)


def params():
    return pltpu.CompilerParams(vmem_limit_bytes=40 * 1024 * 1024)


def cost(flops, moved):
    return pl.CostEstimate(flops=flops, bytes_accessed=moved, transcendentals=0)


def measures_of(operator):
    layers = lax.axis_size("ev")
    measures = operator.shape[0]
    step = layers // 4

    def from_layer(rows, ahead):
        return lax.ppermute(rows, "ev", [((i + ahead) % layers, i) for i in range(layers)])

    far = [operator] + [from_layer(operator, ahead) for ahead in (step, 2 * step, 3 * step)]
    held = jnp.concatenate(far, axis=0)
    parts = [(held, [0, 1, 2, 3], 0)]
    for ahead in (1, -1):
        parts.append((from_layer(held, ahead), [0, 1, 2, 3], ahead))
    for ahead, blocks in ((2, (0, 1)), (-2, (3, 0))):
        some = jnp.concatenate([far[at] for at in blocks], axis=0)
        parts.append((from_layer(some, ahead), blocks, ahead))
    places = [(ahead + step * at) % layers for _, blocks, ahead in parts for at in blocks]
    measure = jnp.arange(layers * measures, dtype=jnp.int32)
    distance = (measure // measures - lax.axis_index("ev")) % layers
    place = sum(jnp.where(distance == far_off, at, 0) for at, far_off in enumerate(places))
    return [rows for rows, _, _ in parts], place * measures + measure % measures


def shards(
    hazard,
    route_tiles,
    block_slots,
    corner_cells,
    corner_weights,
    block_class,
    curves,
    exposure,
    event_ssp,
    operator,
):
    events = hazard.shape[0]
    devices = lax.axis_size("asset")
    slots = route_tiles.shape[1]
    span = corner_cells.shape[1]
    with jax.named_scope("measures"):
        parts, order = measures_of(operator)
    with jax.named_scope("pack"):
        packed = pl.pallas_call(
            pack_kernel,
            out_shape=pltpu.HBM((slots, events, TILE), jnp.bfloat16),
            in_specs=[pl.BlockSpec(memory_space=pltpu.HBM)] * 2,
            out_specs=pl.BlockSpec(memory_space=pltpu.HBM),
            scratch_shapes=[
                pltpu.SMEM((1, slots), jnp.int32),
                pltpu.VMEM(hazard.shape, hazard.dtype),
                pltpu.SemaphoreType.DMA((2,)),
                pltpu.SemaphoreType.DMA((slots,)),
            ],
            cost_estimate=cost(0, 8 * slots * events * TILE),
        )(route_tiles, hazard)
    with jax.named_scope("tiles"):
        tiles = lax.all_to_all(packed.reshape(devices, -1, TILE), "asset", 0, 0)
        tiles = tiles.reshape(slots, events, TILE)
    wide = jnp.pad(curves, ((0, 0), (0, LANES - LEVELS)))
    ssp = jnp.broadcast_to(event_ssp[:, None], (events, LANES))
    with jax.named_scope("pick"):
        impact = pl.pallas_call(
            pick_kernel,
            out_shape=jax.ShapeDtypeStruct((events, span), jnp.float32),
            in_specs=[smem(), smem()] + [vmem()] * 6,
            out_specs=vmem(),
            compiler_params=params(),
            cost_estimate=cost(2 * CORNERS * OVL * TILE * events * span, 2 * slots * events * TILE),
        )(block_slots, block_class, tiles, corner_cells, corner_weights, wide, exposure, ssp)
    with jax.named_scope("product"):
        terms = pl.pallas_call(
            product_kernel,
            out_shape=jax.ShapeDtypeStruct((events, order.shape[0]), jnp.float32),
            in_specs=[vmem()] * (2 + len(parts)),
            out_specs=vmem(),
            compiler_params=params(),
            cost_estimate=cost(4 * events * order.shape[0] * span, 2 * order.shape[0] * span),
        )(impact, order[None], *parts)
    with jax.named_scope("sums"):
        shares = lax.all_to_all(terms[:, None, :], "asset", 0, 0)
        return jnp.sum(shares, axis=0)


def solution(mesh):
    in_specs = (
        P("ev", "asset"),
        P("asset", None),
        P(None, "asset"),
        P(None, "asset"),
        P(None, "asset"),
        P("asset"),
        P(),
        P(None, "asset"),
        P("ev"),
        P("ev", "asset"),
    )
    out_specs = P(("ev", "asset"), None)
    return jax.shard_map(shards, mesh=mesh, in_specs=in_specs, out_specs=out_specs, check_vma=False)
```

```python
import functools
import jax
import jax.numpy as jnp
from jax import lax
from jax.experimental import pallas as pl
from jax.experimental.pallas import tpu as pltpu
from jax.sharding import PartitionSpec as P

TILE = 1024
BLOCK = 256
OVL = 4
CORNERS = 4
SSPS = 3
CLASSES = 16
LEVELS = 16
LANES = 128
SUB = 8
DEPTH = 256
PACK = 16


def pack_kernel(routes_ref, tiles_ref, out_ref, route_ref, hazard_ref, first_sems, sems):
    route = pltpu.make_async_copy(routes_ref, route_ref, first_sems.at[0])
    hazard = pltpu.make_async_copy(tiles_ref, hazard_ref, first_sems.at[1])
    route.start()
    hazard.start()
    route.wait()
    hazard.wait()

    def copy(slot):
        first = pl.multiple_of(route_ref[0, slot] * TILE, TILE)
        return pltpu.make_async_copy(hazard_ref.at[:, pl.ds(first, TILE)], out_ref.at[slot], sems.at[slot])

    @pl.loop(0, out_ref.shape[0])
    def _(slot):
        copy(slot).start()

    @pl.loop(0, out_ref.shape[0])
    def _(slot):
        copy(slot).wait()


def pick_kernel(
    slots_ref, class_ref, tiles_ref, cells_ref, weights_ref, curves_ref, exposure_ref, ssp_ref, out_ref
):
    events = out_ref.shape[0]
    pieces = TILE // DEPTH
    groups = events // SUB
    rows = lax.broadcasted_iota(jnp.int32, (DEPTH, BLOCK), 0).astype(jnp.float32).astype(jnp.bfloat16)

    def one_hot(cell):
        low = jnp.broadcast_to((cell & (DEPTH - 1)).astype(jnp.float32), (PACK, BLOCK)).astype(jnp.bfloat16)
        hits = [
            jnp.where(rows[first : first + PACK] == low, jnp.bfloat16(1), jnp.bfloat16(0))
            for first in range(0, DEPTH, PACK)
        ]
        return jnp.concatenate(hits, axis=0)

    @pl.loop(0, slots_ref.shape[1], unroll=8)
    def _(block):
        assets = pl.ds(pl.multiple_of(block * BLOCK, BLOCK), BLOCK)
        window = [
            tiles_ref[slots_ref[k, block], :, piece * DEPTH : (piece + 1) * DEPTH]
            for k in range(OVL)
            for piece in range(pieces)
        ]
        cells = [cells_ref[pl.ds(corner, 1), assets] for corner in range(CORNERS)]
        picker = jnp.concatenate([one_hot(cell) for cell in cells], axis=1)
        found = jnp.dot(jnp.concatenate(window, axis=0), picker, preferred_element_type=jnp.float32)
        weights = [jnp.broadcast_to(weights_ref[pl.ds(at, 1), assets], (SUB, BLOCK)) for at in range(CORNERS)]
        scale = (LEVELS - 1) / (weights[0] + weights[1] + weights[2] + weights[3])
        place = [jnp.zeros((SUB, BLOCK), jnp.float32)] * groups
        for corner in range(CORNERS):
            high = jnp.broadcast_to(cells[corner], (SUB, BLOCK)) // DEPTH
            mine = found[:, corner * BLOCK : (corner + 1) * BLOCK]
            value = [mine[group * SUB : (group + 1) * SUB] for group in range(groups)]
            for part in range(1, OVL * pieces):
                here = high == part
                for group in range(groups):
                    first = part * events + group * SUB
                    value[group] = jnp.where(here, mine[first : first + SUB], value[group])
            place = [place[group] + weights[corner] * value[group] for group in range(groups)]
        row = class_ref[block]
        curve = jnp.broadcast_to(curves_ref[pl.ds(row, 1), :], (SUB, LANES))
        values = [jnp.broadcast_to(exposure_ref[pl.ds(at, 1), assets], (SUB, BLOCK)) for at in range(SSPS)]
        for group in range(groups):
            lines = slice(group * SUB, (group + 1) * SUB)
            spot = place[group] * scale
            level = jnp.clip(spot.astype(jnp.int32), 0, LEVELS - 2)
            part = spot - level.astype(jnp.float32)
            base, top = [], []
            for half in range(BLOCK // LANES):
                here = level[:, half * LANES : (half + 1) * LANES]
                base.append(jnp.take_along_axis(curve, here, axis=1, mode="promise_in_bounds"))
                top.append(jnp.take_along_axis(curve, here + 1, axis=1, mode="promise_in_bounds"))
            base, top = jnp.concatenate(base, axis=1), jnp.concatenate(top, axis=1)
            scenario = jnp.concatenate([ssp_ref[lines, :]] * (BLOCK // LANES), axis=1)
            value = jnp.where(scenario == 0, values[0], jnp.where(scenario == 1, values[1], values[2]))
            out_ref[lines, assets] = value * (base * (1.0 - part) + top * part)


def product_kernel(impact_ref, order_ref, *refs):
    *rows_refs, out_ref = refs
    step = 512
    events = impact_ref.shape[0]
    dims = (((1,), (1,)), ((), ()))
    total = jnp.zeros(out_ref.shape, jnp.float32)
    for first in range(0, impact_ref.shape[1], step):
        impact = impact_ref[:, first : first + step]
        rows = jnp.concatenate([ref[:, first : first + step] for ref in rows_refs], axis=0)
        top = impact.astype(jnp.bfloat16)
        rest = (impact - top.astype(jnp.float32)).astype(jnp.bfloat16)
        both = jnp.concatenate([top, rest], axis=0)
        sums = lax.dot_general(both, rows, dims, preferred_element_type=jnp.float32)
        total = total + (sums[:events] + sums[events:])
    order = jnp.broadcast_to(order_ref[...], total.shape)
    out_ref[...] = jnp.take_along_axis(total, order, axis=1, mode="promise_in_bounds")


def vmem():
    return pl.BlockSpec(memory_space=pltpu.VMEM)


def smem():
    return pl.BlockSpec(memory_space=pltpu.SMEM)


def params():
    return pltpu.CompilerParams(vmem_limit_bytes=40 * 1024 * 1024)


def cost(flops, moved):
    return pl.CostEstimate(flops=flops, bytes_accessed=moved, transcendentals=0)


def measures_of(operator):
    layers = lax.axis_size("ev")
    measures = operator.shape[0]
    step = layers // 4

    def from_layer(rows, ahead):
        return lax.ppermute(rows, "ev", [((i + ahead) % layers, i) for i in range(layers)])

    far = [operator] + [from_layer(operator, ahead) for ahead in (step, 2 * step, 3 * step)]
    held = jnp.concatenate(far, axis=0)
    parts = [(held, [0, 1, 2, 3], 0)]
    for ahead in (1, -1):
        parts.append((from_layer(held, ahead), [0, 1, 2, 3], ahead))
    for ahead, blocks in ((2, (0, 1)), (-2, (3, 0))):
        some = jnp.concatenate([far[at] for at in blocks], axis=0)
        parts.append((from_layer(some, ahead), blocks, ahead))
    places = [(ahead + step * at) % layers for _, blocks, ahead in parts for at in blocks]
    measure = jnp.arange(layers * measures, dtype=jnp.int32)
    distance = (measure // measures - lax.axis_index("ev")) % layers
    place = sum(jnp.where(distance == far_off, at, 0) for at, far_off in enumerate(places))
    return [rows for rows, _, _ in parts], place * measures + measure % measures


def shards(
    hazard,
    route_tiles,
    block_slots,
    corner_cells,
    corner_weights,
    block_class,
    curves,
    exposure,
    event_ssp,
    operator,
):
    events = hazard.shape[0]
    devices = lax.axis_size("asset")
    slots = route_tiles.shape[1]
    span = corner_cells.shape[1]
    with jax.named_scope("measures"):
        parts, order = measures_of(operator)
    with jax.named_scope("pack"):
        packed = pl.pallas_call(
            pack_kernel,
            out_shape=pltpu.HBM((slots, events, TILE), jnp.bfloat16),
            in_specs=[pl.BlockSpec(memory_space=pltpu.HBM)] * 2,
            out_specs=pl.BlockSpec(memory_space=pltpu.HBM),
            scratch_shapes=[
                pltpu.SMEM((1, slots), jnp.int32),
                pltpu.VMEM(hazard.shape, hazard.dtype),
                pltpu.SemaphoreType.DMA((2,)),
                pltpu.SemaphoreType.DMA((slots,)),
            ],
            cost_estimate=cost(0, 8 * slots * events * TILE),
        )(route_tiles, hazard)
    with jax.named_scope("tiles"):
        tiles = lax.all_to_all(packed.reshape(devices, -1, TILE), "asset", 0, 0)
        tiles = tiles.reshape(slots, events, TILE)
    wide = jnp.pad(curves, ((0, 0), (0, LANES - LEVELS)))
    ssp = jnp.broadcast_to(event_ssp[:, None], (events, LANES))
    with jax.named_scope("pick"):
        impact = pl.pallas_call(
            pick_kernel,
            out_shape=jax.ShapeDtypeStruct((events, span), jnp.float32),
            in_specs=[smem(), smem()] + [vmem()] * 6,
            out_specs=vmem(),
            compiler_params=params(),
            cost_estimate=cost(2 * CORNERS * OVL * TILE * events * span, 2 * slots * events * TILE),
        )(block_slots, block_class, tiles, corner_cells, corner_weights, wide, exposure, ssp)
    with jax.named_scope("product"):
        terms = pl.pallas_call(
            product_kernel,
            out_shape=jax.ShapeDtypeStruct((events, order.shape[0]), jnp.float32),
            in_specs=[vmem()] * (2 + len(parts)),
            out_specs=vmem(),
            compiler_params=params(),
            cost_estimate=cost(4 * events * order.shape[0] * span, 2 * order.shape[0] * span),
        )(impact, order[None], *parts)
    with jax.named_scope("sums"):
        shares = lax.all_to_all(terms[:, None, :], "asset", 0, 0)
        return jnp.sum(shares, axis=0)


def solution(mesh):
    in_specs = (
        P("ev", "asset"),
        P("asset", None),
        P(None, "asset"),
        P(None, "asset"),
        P(None, "asset"),
        P("asset"),
        P(),
        P(None, "asset"),
        P("ev"),
        P("ev", "asset"),
    )
    out_specs = P(("ev", "asset"), None)
    return jax.shard_map(shards, mesh=mesh, in_specs=in_specs, out_specs=out_specs, check_vma=False)
```

```python
import functools
import jax
import jax.numpy as jnp
from jax import lax
from jax.experimental import pallas as pl
from jax.experimental.pallas import tpu as pltpu
from jax.sharding import PartitionSpec as P

TILE = 1024
BLOCK = 256
OVL = 4
CAP = 2
CORES = 2
CORNERS = 4
SSPS = 3
CLASSES = 16
LEVELS = 16
LANES = 128
SUB = 8
DEPTH = 256
PACK = 16


def turned(slot, slots):
    inner = CORES * CAP
    bits = ((slots // inner).bit_length() - 1) // 2
    chip = slot >> (inner.bit_length() - 1)
    return (((chip & ((1 << bits) - 1)) << bits) + (chip >> bits)) * inner + (slot & (inner - 1))


def pack_kernel(routes_ref, tiles_ref, out_ref, route_ref, hazard_ref, first_sems, sems):
    slots = out_ref.shape[0]
    route = pltpu.make_async_copy(routes_ref, route_ref, first_sems.at[0])
    hazard = pltpu.make_async_copy(tiles_ref, hazard_ref, first_sems.at[1])
    route.start()
    hazard.start()
    route.wait()
    hazard.wait()

    def copy(slot):
        first = pl.multiple_of(route_ref[0, turned(slot, slots)] * TILE, TILE)
        return pltpu.make_async_copy(hazard_ref.at[:, pl.ds(first, TILE)], out_ref.at[slot], sems.at[slot])

    @pl.loop(0, out_ref.shape[0])
    def _(slot):
        copy(slot).start()

    @pl.loop(0, out_ref.shape[0])
    def _(slot):
        copy(slot).wait()


def pick_kernel(
    slots_ref, class_ref, tiles_ref, cells_ref, weights_ref, curves_ref, exposure_ref, ssp_ref, out_ref
):
    events = out_ref.shape[0]
    slots = tiles_ref.shape[0]
    pieces = TILE // DEPTH
    groups = events // SUB
    rows = lax.broadcasted_iota(jnp.int32, (DEPTH, BLOCK), 0).astype(jnp.float32).astype(jnp.bfloat16)

    def one_hot(cell):
        low = jnp.broadcast_to((cell & (DEPTH - 1)).astype(jnp.float32), (PACK, BLOCK)).astype(jnp.bfloat16)
        hits = [
            jnp.where(rows[first : first + PACK] == low, jnp.bfloat16(1), jnp.bfloat16(0))
            for first in range(0, DEPTH, PACK)
        ]
        return jnp.concatenate(hits, axis=0)

    @pl.loop(0, slots_ref.shape[1], unroll=8)
    def _(block):
        assets = pl.ds(pl.multiple_of(block * BLOCK, BLOCK), BLOCK)
        window = [
            tiles_ref[turned(slots_ref[k, block], slots), :, piece * DEPTH : (piece + 1) * DEPTH]
            for k in range(OVL)
            for piece in range(pieces)
        ]
        cells = [cells_ref[pl.ds(corner, 1), assets] for corner in range(CORNERS)]
        picker = jnp.concatenate([one_hot(cell) for cell in cells], axis=1)
        found = jnp.dot(jnp.concatenate(window, axis=0), picker, preferred_element_type=jnp.float32)
        weights = [jnp.broadcast_to(weights_ref[pl.ds(at, 1), assets], (SUB, BLOCK)) for at in range(CORNERS)]
        scale = (LEVELS - 1) / (weights[0] + weights[1] + weights[2] + weights[3])
        place = [jnp.zeros((SUB, BLOCK), jnp.float32)] * groups
        for corner in range(CORNERS):
            high = jnp.broadcast_to(cells[corner], (SUB, BLOCK)) // DEPTH
            mine = found[:, corner * BLOCK : (corner + 1) * BLOCK]
            value = [mine[group * SUB : (group + 1) * SUB] for group in range(groups)]
            for part in range(1, OVL * pieces):
                here = high == part
                for group in range(groups):
                    first = part * events + group * SUB
                    value[group] = jnp.where(here, mine[first : first + SUB], value[group])
            place = [place[group] + weights[corner] * value[group] for group in range(groups)]
        row = class_ref[block]
        curve = jnp.broadcast_to(curves_ref[pl.ds(row, 1), :], (SUB, LANES))
        values = [jnp.broadcast_to(exposure_ref[pl.ds(at, 1), assets], (SUB, BLOCK)) for at in range(SSPS)]
        for group in range(groups):
            lines = slice(group * SUB, (group + 1) * SUB)
            spot = place[group] * scale
            level = jnp.clip(spot.astype(jnp.int32), 0, LEVELS - 2)
            part = spot - level.astype(jnp.float32)
            base, top = [], []
            for half in range(BLOCK // LANES):
                here = level[:, half * LANES : (half + 1) * LANES]
                base.append(jnp.take_along_axis(curve, here, axis=1, mode="promise_in_bounds"))
                top.append(jnp.take_along_axis(curve, here + 1, axis=1, mode="promise_in_bounds"))
            base, top = jnp.concatenate(base, axis=1), jnp.concatenate(top, axis=1)
            scenario = jnp.concatenate([ssp_ref[lines, :]] * (BLOCK // LANES), axis=1)
            value = jnp.where(scenario == 0, values[0], jnp.where(scenario == 1, values[1], values[2]))
            out_ref[lines, assets] = value * (base * (1.0 - part) + top * part)


def product_kernel(impact_ref, order_ref, *refs):
    *rows_refs, out_ref = refs
    step = 512
    events = impact_ref.shape[0]
    dims = (((1,), (1,)), ((), ()))
    total = jnp.zeros(out_ref.shape, jnp.float32)
    for first in range(0, impact_ref.shape[1], step):
        impact = impact_ref[:, first : first + step]
        rows = jnp.concatenate([ref[:, first : first + step] for ref in rows_refs], axis=0)
        top = impact.astype(jnp.bfloat16)
        rest = (impact - top.astype(jnp.float32)).astype(jnp.bfloat16)
        both = jnp.concatenate([top, rest], axis=0)
        sums = lax.dot_general(both, rows, dims, preferred_element_type=jnp.float32)
        total = total + (sums[:events] + sums[events:])
    order = jnp.broadcast_to(order_ref[...], total.shape)
    out_ref[...] = jnp.take_along_axis(total, order, axis=1, mode="promise_in_bounds")


def vmem():
    return pl.BlockSpec(memory_space=pltpu.VMEM)


def smem():
    return pl.BlockSpec(memory_space=pltpu.SMEM)


def params():
    return pltpu.CompilerParams(vmem_limit_bytes=40 * 1024 * 1024)


def cost(flops, moved):
    return pl.CostEstimate(flops=flops, bytes_accessed=moved, transcendentals=0)


def measures_of(operator):
    layers = lax.axis_size("ev")
    measures = operator.shape[0]
    step = layers // 4

    def from_layer(rows, ahead):
        return lax.ppermute(rows, "ev", [((i + ahead) % layers, i) for i in range(layers)])

    far = [operator] + [from_layer(operator, ahead) for ahead in (step, 2 * step, 3 * step)]
    held = jnp.concatenate(far, axis=0)
    parts = [(held, [0, 1, 2, 3], 0)]
    for ahead in (1, -1):
        parts.append((from_layer(held, ahead), [0, 1, 2, 3], ahead))
    for ahead, blocks in ((2, (0, 1)), (-2, (3, 0))):
        some = jnp.concatenate([far[at] for at in blocks], axis=0)
        parts.append((from_layer(some, ahead), blocks, ahead))
    places = [(ahead + step * at) % layers for _, blocks, ahead in parts for at in blocks]
    measure = jnp.arange(layers * measures, dtype=jnp.int32)
    distance = (measure // measures - lax.axis_index("ev")) % layers
    place = sum(jnp.where(distance == far_off, at, 0) for at, far_off in enumerate(places))
    return [rows for rows, _, _ in parts], place * measures + measure % measures


def shards(
    hazard,
    route_tiles,
    block_slots,
    corner_cells,
    corner_weights,
    block_class,
    curves,
    exposure,
    event_ssp,
    operator,
):
    events = hazard.shape[0]
    devices = lax.axis_size("asset")
    slots = route_tiles.shape[1]
    span = corner_cells.shape[1]
    with jax.named_scope("measures"):
        parts, order = measures_of(operator)
    with jax.named_scope("pack"):
        packed = pl.pallas_call(
            pack_kernel,
            out_shape=pltpu.HBM((slots, events, TILE), jnp.bfloat16),
            in_specs=[pl.BlockSpec(memory_space=pltpu.HBM)] * 2,
            out_specs=pl.BlockSpec(memory_space=pltpu.HBM),
            scratch_shapes=[
                pltpu.SMEM((1, slots), jnp.int32),
                pltpu.VMEM(hazard.shape, hazard.dtype),
                pltpu.SemaphoreType.DMA((2,)),
                pltpu.SemaphoreType.DMA((slots,)),
            ],
            cost_estimate=cost(0, 8 * slots * events * TILE),
        )(route_tiles, hazard)
    with jax.named_scope("tiles"):
        listed = [turned(CAP * device, slots) // CAP for device in range(devices)]
        packed = packed.reshape(devices, -1, TILE)
        tiles = lax.all_to_all(packed, "asset", 0, 0, axis_index_groups=[listed])
        tiles = tiles.reshape(slots, events, TILE)
    wide = jnp.pad(curves, ((0, 0), (0, LANES - LEVELS)))
    ssp = jnp.broadcast_to(event_ssp[:, None], (events, LANES))
    with jax.named_scope("pick"):
        impact = pl.pallas_call(
            pick_kernel,
            out_shape=jax.ShapeDtypeStruct((events, span), jnp.float32),
            in_specs=[smem(), smem()] + [vmem()] * 6,
            out_specs=vmem(),
            compiler_params=params(),
            cost_estimate=cost(2 * CORNERS * OVL * TILE * events * span, 2 * slots * events * TILE),
        )(block_slots, block_class, tiles, corner_cells, corner_weights, wide, exposure, ssp)
    with jax.named_scope("product"):
        terms = pl.pallas_call(
            product_kernel,
            out_shape=jax.ShapeDtypeStruct((events, order.shape[0]), jnp.float32),
            in_specs=[vmem()] * (2 + len(parts)),
            out_specs=vmem(),
            compiler_params=params(),
            cost_estimate=cost(4 * events * order.shape[0] * span, 2 * order.shape[0] * span),
        )(impact, order[None], *parts)
    with jax.named_scope("sums"):
        shares = lax.all_to_all(terms[:, None, :], "asset", 0, 0)
        return jnp.sum(shares, axis=0)


def solution(mesh):
    in_specs = (
        P("ev", "asset"),
        P("asset", None),
        P(None, "asset"),
        P(None, "asset"),
        P(None, "asset"),
        P("asset"),
        P(),
        P(None, "asset"),
        P("ev"),
        P("ev", "asset"),
    )
    out_specs = P(("ev", "asset"), None)
    return jax.shard_map(shards, mesh=mesh, in_specs=in_specs, out_specs=out_specs, check_vma=False)
```

```python
import functools
import jax
import jax.numpy as jnp
from jax import lax
from jax.experimental import pallas as pl
from jax.experimental.pallas import tpu as pltpu
from jax.sharding import PartitionSpec as P

TILE = 1024
BLOCK = 256
OVL = 4
CAP = 2
CORES = 2
CORNERS = 4
SSPS = 3
CLASSES = 16
LEVELS = 16
LANES = 128
SUB = 8
DEPTH = 256
PACK = 16


def turned(slot, slots):
    inner = CORES * CAP
    bits = ((slots // inner).bit_length() - 1) // 2
    chip = slot >> (inner.bit_length() - 1)
    return (((chip & ((1 << bits) - 1)) << bits) + (chip >> bits)) * inner + (slot & (inner - 1))


def pack_kernel(routes_ref, tiles_ref, out_ref, route_ref, hazard_ref, first_sems, sems):
    slots = out_ref.shape[0]
    route = pltpu.make_async_copy(routes_ref, route_ref, first_sems.at[0])
    hazard = pltpu.make_async_copy(tiles_ref, hazard_ref, first_sems.at[1])
    route.start()
    hazard.start()
    route.wait()
    hazard.wait()

    def copy(slot):
        first = pl.multiple_of(route_ref[0, turned(slot, slots)] * TILE, TILE)
        return pltpu.make_async_copy(hazard_ref.at[:, pl.ds(first, TILE)], out_ref.at[slot], sems.at[slot])

    @pl.loop(0, out_ref.shape[0])
    def _(slot):
        copy(slot).start()

    @pl.loop(0, out_ref.shape[0])
    def _(slot):
        copy(slot).wait()


def pick_kernel(
    slots_ref, class_ref, tiles_ref, cells_ref, weights_ref, curves_ref, exposure_ref, ssp_ref, out_ref
):
    events = out_ref.shape[0]
    slots = tiles_ref.shape[0]
    pieces = TILE // DEPTH
    groups = events // SUB
    rows = lax.broadcasted_iota(jnp.int32, (DEPTH, BLOCK), 0).astype(jnp.float32).astype(jnp.bfloat16)

    def one_hot(cell):
        low = jnp.broadcast_to((cell & (DEPTH - 1)).astype(jnp.float32), (PACK, BLOCK)).astype(jnp.bfloat16)
        hits = [
            jnp.where(rows[first : first + PACK] == low, jnp.bfloat16(1), jnp.bfloat16(0))
            for first in range(0, DEPTH, PACK)
        ]
        return jnp.concatenate(hits, axis=0)

    @pl.loop(0, slots_ref.shape[1], unroll=16)
    def _(block):
        assets = pl.ds(pl.multiple_of(block * BLOCK, BLOCK), BLOCK)
        window = [
            tiles_ref[turned(slots_ref[k, block], slots), :, piece * DEPTH : (piece + 1) * DEPTH]
            for k in range(OVL)
            for piece in range(pieces)
        ]
        cells = [cells_ref[pl.ds(corner, 1), assets] for corner in range(CORNERS)]
        picker = jnp.concatenate([one_hot(cell) for cell in cells], axis=1)
        found = jnp.dot(jnp.concatenate(window, axis=0), picker, preferred_element_type=jnp.float32)
        weights = [jnp.broadcast_to(weights_ref[pl.ds(at, 1), assets], (SUB, BLOCK)) for at in range(CORNERS)]
        scale = (LEVELS - 1) / (weights[0] + weights[1] + weights[2] + weights[3])
        place = [jnp.zeros((SUB, BLOCK), jnp.float32)] * groups
        for corner in range(CORNERS):
            high = jnp.broadcast_to(cells[corner], (SUB, BLOCK)) // DEPTH
            mine = found[:, corner * BLOCK : (corner + 1) * BLOCK]
            value = [mine[group * SUB : (group + 1) * SUB] for group in range(groups)]
            for part in range(1, OVL * pieces):
                here = high == part
                for group in range(groups):
                    first = part * events + group * SUB
                    value[group] = jnp.where(here, mine[first : first + SUB], value[group])
            place = [place[group] + weights[corner] * value[group] for group in range(groups)]
        row = class_ref[block]
        curve = jnp.broadcast_to(curves_ref[pl.ds(row, 1), :], (SUB, LANES))
        values = [jnp.broadcast_to(exposure_ref[pl.ds(at, 1), assets], (SUB, BLOCK)) for at in range(SSPS)]
        for group in range(groups):
            lines = slice(group * SUB, (group + 1) * SUB)
            spot = place[group] * scale
            level = jnp.clip(spot.astype(jnp.int32), 0, LEVELS - 2)
            part = spot - level.astype(jnp.float32)
            base, top = [], []
            for half in range(BLOCK // LANES):
                here = level[:, half * LANES : (half + 1) * LANES]
                base.append(jnp.take_along_axis(curve, here, axis=1, mode="promise_in_bounds"))
                top.append(jnp.take_along_axis(curve, here + 1, axis=1, mode="promise_in_bounds"))
            base, top = jnp.concatenate(base, axis=1), jnp.concatenate(top, axis=1)
            scenario = jnp.concatenate([ssp_ref[lines, :]] * (BLOCK // LANES), axis=1)
            value = jnp.where(scenario == 0, values[0], jnp.where(scenario == 1, values[1], values[2]))
            out_ref[lines, assets] = value * (base * (1.0 - part) + top * part)


def product_kernel(impact_ref, order_ref, *refs):
    *rows_refs, out_ref = refs
    step = 512
    events = impact_ref.shape[0]
    dims = (((1,), (1,)), ((), ()))
    total = jnp.zeros(out_ref.shape, jnp.float32)
    for first in range(0, impact_ref.shape[1], step):
        impact = impact_ref[:, first : first + step]
        rows = jnp.concatenate([ref[:, first : first + step] for ref in rows_refs], axis=0)
        top = impact.astype(jnp.bfloat16)
        rest = (impact - top.astype(jnp.float32)).astype(jnp.bfloat16)
        both = jnp.concatenate([top, rest], axis=0)
        sums = lax.dot_general(both, rows, dims, preferred_element_type=jnp.float32)
        total = total + (sums[:events] + sums[events:])
    order = jnp.broadcast_to(order_ref[...], total.shape)
    out_ref[...] = jnp.take_along_axis(total, order, axis=1, mode="promise_in_bounds")


def vmem():
    return pl.BlockSpec(memory_space=pltpu.VMEM)


def smem():
    return pl.BlockSpec(memory_space=pltpu.SMEM)


def params():
    return pltpu.CompilerParams(vmem_limit_bytes=40 * 1024 * 1024)


def cost(flops, moved):
    return pl.CostEstimate(flops=flops, bytes_accessed=moved, transcendentals=0)


def measures_of(operator):
    layers = lax.axis_size("ev")
    measures = operator.shape[0]
    step = layers // 4

    def from_layer(rows, ahead):
        return lax.ppermute(rows, "ev", [((i + ahead) % layers, i) for i in range(layers)])

    far = [operator] + [from_layer(operator, ahead) for ahead in (step, 2 * step, 3 * step)]
    held = jnp.concatenate(far, axis=0)
    parts = [(held, [0, 1, 2, 3], 0)]
    for ahead in (1, -1):
        parts.append((from_layer(held, ahead), [0, 1, 2, 3], ahead))
    for ahead, blocks in ((2, (0, 1)), (-2, (3, 0))):
        some = jnp.concatenate([far[at] for at in blocks], axis=0)
        parts.append((from_layer(some, ahead), blocks, ahead))
    places = [(ahead + step * at) % layers for _, blocks, ahead in parts for at in blocks]
    measure = jnp.arange(layers * measures, dtype=jnp.int32)
    distance = (measure // measures - lax.axis_index("ev")) % layers
    place = sum(jnp.where(distance == far_off, at, 0) for at, far_off in enumerate(places))
    return [rows for rows, _, _ in parts], place * measures + measure % measures


def shards(
    hazard,
    route_tiles,
    block_slots,
    corner_cells,
    corner_weights,
    block_class,
    curves,
    exposure,
    event_ssp,
    operator,
):
    events = hazard.shape[0]
    devices = lax.axis_size("asset")
    slots = route_tiles.shape[1]
    span = corner_cells.shape[1]
    with jax.named_scope("measures"):
        parts, order = measures_of(operator)
    with jax.named_scope("pack"):
        packed = pl.pallas_call(
            pack_kernel,
            out_shape=pltpu.HBM((slots, events, TILE), jnp.bfloat16),
            in_specs=[pl.BlockSpec(memory_space=pltpu.HBM)] * 2,
            out_specs=pl.BlockSpec(memory_space=pltpu.HBM),
            scratch_shapes=[
                pltpu.SMEM((1, slots), jnp.int32),
                pltpu.VMEM(hazard.shape, hazard.dtype),
                pltpu.SemaphoreType.DMA((2,)),
                pltpu.SemaphoreType.DMA((slots,)),
            ],
            cost_estimate=cost(0, 8 * slots * events * TILE),
        )(route_tiles, hazard)
    with jax.named_scope("tiles"):
        listed = [turned(CAP * device, slots) // CAP for device in range(devices)]
        packed = packed.reshape(devices, -1, TILE)
        tiles = lax.all_to_all(packed, "asset", 0, 0, axis_index_groups=[listed])
        tiles = tiles.reshape(slots, events, TILE)
    wide = jnp.pad(curves, ((0, 0), (0, LANES - LEVELS)))
    ssp = jnp.broadcast_to(event_ssp[:, None], (events, LANES))
    with jax.named_scope("pick"):
        impact = pl.pallas_call(
            pick_kernel,
            out_shape=jax.ShapeDtypeStruct((events, span), jnp.float32),
            in_specs=[smem(), smem()] + [vmem()] * 6,
            out_specs=vmem(),
            compiler_params=params(),
            cost_estimate=cost(2 * CORNERS * OVL * TILE * events * span, 2 * slots * events * TILE),
        )(block_slots, block_class, tiles, corner_cells, corner_weights, wide, exposure, ssp)
    with jax.named_scope("product"):
        terms = pl.pallas_call(
            product_kernel,
            out_shape=jax.ShapeDtypeStruct((events, order.shape[0]), jnp.float32),
            in_specs=[vmem()] * (2 + len(parts)),
            out_specs=vmem(),
            compiler_params=params(),
            cost_estimate=cost(4 * events * order.shape[0] * span, 2 * order.shape[0] * span),
        )(impact, order[None], *parts)
    with jax.named_scope("sums"):
        shares = lax.all_to_all(terms[:, None, :], "asset", 0, 0)
        return jnp.sum(shares, axis=0)


def solution(mesh):
    in_specs = (
        P("ev", "asset"),
        P("asset", None),
        P(None, "asset"),
        P(None, "asset"),
        P(None, "asset"),
        P("asset"),
        P(),
        P(None, "asset"),
        P("ev"),
        P("ev", "asset"),
    )
    out_specs = P(("ev", "asset"), None)
    return jax.shard_map(shards, mesh=mesh, in_specs=in_specs, out_specs=out_specs, check_vma=False)
```

```python
import functools
import jax
import jax.numpy as jnp
from jax import lax
from jax.experimental import pallas as pl
from jax.experimental.pallas import tpu as pltpu
from jax.sharding import PartitionSpec as P

TILE = 1024
BLOCK = 256
OVL = 4
CAP = 2
CORNERS = 4
SSPS = 3
CLASSES = 16
LEVELS = 16
LANES = 128
SUB = 8
DEPTH = 256
PACK = 16


def slot_at(place):
    return ((place >> 1) & 3) * 16 + (place >> 4) * 4 + ((place >> 3) & 1) * 2 + (place & 1)


def place_of(slot):
    return ((slot >> 2) & 3) * 16 + ((slot >> 1) & 1) * 8 + (slot >> 4) * 2 + (slot & 1)


def pack_kernel(routes_ref, tiles_ref, out_ref, route_ref, hazard_ref, first_sems, sems):
    route = pltpu.make_async_copy(routes_ref, route_ref, first_sems.at[0])
    hazard = pltpu.make_async_copy(tiles_ref, hazard_ref, first_sems.at[1])
    route.start()
    hazard.start()
    route.wait()
    hazard.wait()

    def copy(slot):
        first = pl.multiple_of(route_ref[0, slot_at(slot)] * TILE, TILE)
        return pltpu.make_async_copy(hazard_ref.at[:, pl.ds(first, TILE)], out_ref.at[slot], sems.at[slot])

    @pl.loop(0, out_ref.shape[0])
    def _(slot):
        copy(slot).start()

    @pl.loop(0, out_ref.shape[0])
    def _(slot):
        copy(slot).wait()


def pick_kernel(
    slots_ref, class_ref, tiles_ref, cells_ref, weights_ref, curves_ref, exposure_ref, ssp_ref, out_ref
):
    events = out_ref.shape[0]
    pieces = TILE // DEPTH
    groups = events // SUB
    rows = lax.broadcasted_iota(jnp.int32, (DEPTH, BLOCK), 0).astype(jnp.float32).astype(jnp.bfloat16)

    def one_hot(cell):
        low = jnp.broadcast_to((cell & (DEPTH - 1)).astype(jnp.float32), (PACK, BLOCK)).astype(jnp.bfloat16)
        hits = [
            jnp.where(rows[first : first + PACK] == low, jnp.bfloat16(1), jnp.bfloat16(0))
            for first in range(0, DEPTH, PACK)
        ]
        return jnp.concatenate(hits, axis=0)

    @pl.loop(0, slots_ref.shape[1], unroll=16)
    def _(block):
        assets = pl.ds(pl.multiple_of(block * BLOCK, BLOCK), BLOCK)
        window = [
            tiles_ref[place_of(slots_ref[k, block]), :, piece * DEPTH : (piece + 1) * DEPTH]
            for k in range(OVL)
            for piece in range(pieces)
        ]
        cells = [cells_ref[pl.ds(corner, 1), assets] for corner in range(CORNERS)]
        picker = jnp.concatenate([one_hot(cell) for cell in cells], axis=1)
        found = jnp.dot(jnp.concatenate(window, axis=0), picker, preferred_element_type=jnp.float32)
        weights = [jnp.broadcast_to(weights_ref[pl.ds(at, 1), assets], (SUB, BLOCK)) for at in range(CORNERS)]
        scale = (LEVELS - 1) / (weights[0] + weights[1] + weights[2] + weights[3])
        place = [jnp.zeros((SUB, BLOCK), jnp.float32)] * groups
        for corner in range(CORNERS):
            high = jnp.broadcast_to(cells[corner], (SUB, BLOCK)) // DEPTH
            mine = found[:, corner * BLOCK : (corner + 1) * BLOCK]
            value = [mine[group * SUB : (group + 1) * SUB] for group in range(groups)]
            for part in range(1, OVL * pieces):
                here = high == part
                for group in range(groups):
                    first = part * events + group * SUB
                    value[group] = jnp.where(here, mine[first : first + SUB], value[group])
            place = [place[group] + weights[corner] * value[group] for group in range(groups)]
        row = class_ref[block]
        curve = jnp.broadcast_to(curves_ref[pl.ds(row, 1), :], (SUB, LANES))
        values = [jnp.broadcast_to(exposure_ref[pl.ds(at, 1), assets], (SUB, BLOCK)) for at in range(SSPS)]
        for group in range(groups):
            lines = slice(group * SUB, (group + 1) * SUB)
            spot = place[group] * scale
            level = jnp.clip(spot.astype(jnp.int32), 0, LEVELS - 2)
            part = spot - level.astype(jnp.float32)
            base, top = [], []
            for half in range(BLOCK // LANES):
                here = level[:, half * LANES : (half + 1) * LANES]
                base.append(jnp.take_along_axis(curve, here, axis=1, mode="promise_in_bounds"))
                top.append(jnp.take_along_axis(curve, here + 1, axis=1, mode="promise_in_bounds"))
            base, top = jnp.concatenate(base, axis=1), jnp.concatenate(top, axis=1)
            scenario = jnp.concatenate([ssp_ref[lines, :]] * (BLOCK // LANES), axis=1)
            value = jnp.where(scenario == 0, values[0], jnp.where(scenario == 1, values[1], values[2]))
            out_ref[lines, assets] = value * (base * (1.0 - part) + top * part)


def product_kernel(impact_ref, order_ref, *refs):
    *rows_refs, out_ref = refs
    step = 512
    events = impact_ref.shape[0]
    dims = (((1,), (1,)), ((), ()))
    total = jnp.zeros(out_ref.shape, jnp.float32)
    for first in range(0, impact_ref.shape[1], step):
        impact = impact_ref[:, first : first + step]
        rows = jnp.concatenate([ref[:, first : first + step] for ref in rows_refs], axis=0)
        top = impact.astype(jnp.bfloat16)
        rest = (impact - top.astype(jnp.float32)).astype(jnp.bfloat16)
        both = jnp.concatenate([top, rest], axis=0)
        sums = lax.dot_general(both, rows, dims, preferred_element_type=jnp.float32)
        total = total + (sums[:events] + sums[events:])
    order = jnp.broadcast_to(order_ref[...], total.shape)
    out_ref[...] = jnp.take_along_axis(total, order, axis=1, mode="promise_in_bounds")


def vmem():
    return pl.BlockSpec(memory_space=pltpu.VMEM)


def smem():
    return pl.BlockSpec(memory_space=pltpu.SMEM)


def params():
    return pltpu.CompilerParams(vmem_limit_bytes=40 * 1024 * 1024)


def cost(flops, moved):
    return pl.CostEstimate(flops=flops, bytes_accessed=moved, transcendentals=0)


def measures_of(operator):
    layers = lax.axis_size("ev")
    measures = operator.shape[0]
    step = layers // 4

    def from_layer(rows, ahead):
        return lax.ppermute(rows, "ev", [((i + ahead) % layers, i) for i in range(layers)])

    far = [operator] + [from_layer(operator, ahead) for ahead in (step, 2 * step, 3 * step)]
    held = jnp.concatenate(far, axis=0)
    parts = [(held, [0, 1, 2, 3], 0)]
    for ahead in (1, -1):
        parts.append((from_layer(held, ahead), [0, 1, 2, 3], ahead))
    for ahead, blocks in ((2, (0, 1)), (-2, (3, 0))):
        some = jnp.concatenate([far[at] for at in blocks], axis=0)
        parts.append((from_layer(some, ahead), blocks, ahead))
    places = [(ahead + step * at) % layers for _, blocks, ahead in parts for at in blocks]
    measure = jnp.arange(layers * measures, dtype=jnp.int32)
    distance = (measure // measures - lax.axis_index("ev")) % layers
    place = sum(jnp.where(distance == far_off, at, 0) for at, far_off in enumerate(places))
    return [rows for rows, _, _ in parts], place * measures + measure % measures


def shards(
    hazard,
    route_tiles,
    block_slots,
    corner_cells,
    corner_weights,
    block_class,
    curves,
    exposure,
    event_ssp,
    operator,
):
    events = hazard.shape[0]
    devices = lax.axis_size("asset")
    slots = route_tiles.shape[1]
    span = corner_cells.shape[1]
    with jax.named_scope("measures"):
        parts, order = measures_of(operator)
    with jax.named_scope("pack"):
        packed = pl.pallas_call(
            pack_kernel,
            out_shape=pltpu.HBM((slots, events, TILE), jnp.bfloat16),
            in_specs=[pl.BlockSpec(memory_space=pltpu.HBM)] * 2,
            out_specs=pl.BlockSpec(memory_space=pltpu.HBM),
            scratch_shapes=[
                pltpu.SMEM((1, slots), jnp.int32),
                pltpu.VMEM(hazard.shape, hazard.dtype),
                pltpu.SemaphoreType.DMA((2,)),
                pltpu.SemaphoreType.DMA((slots,)),
            ],
            cost_estimate=cost(0, 8 * slots * events * TILE),
        )(route_tiles, hazard)
    with jax.named_scope("tiles"):
        listed = [slot_at(CAP * at) // CAP for at in range(devices)]
        packed = packed.reshape(devices, -1, TILE)
        tiles = lax.all_to_all(packed, "asset", 0, 0, axis_index_groups=[listed])
        tiles = tiles.reshape(slots, events, TILE)
    wide = jnp.pad(curves, ((0, 0), (0, LANES - LEVELS)))
    ssp = jnp.broadcast_to(event_ssp[:, None], (events, LANES))
    with jax.named_scope("pick"):
        impact = pl.pallas_call(
            pick_kernel,
            out_shape=jax.ShapeDtypeStruct((events, span), jnp.float32),
            in_specs=[smem(), smem()] + [vmem()] * 6,
            out_specs=vmem(),
            compiler_params=params(),
            cost_estimate=cost(2 * CORNERS * OVL * TILE * events * span, 2 * slots * events * TILE),
        )(block_slots, block_class, tiles, corner_cells, corner_weights, wide, exposure, ssp)
    with jax.named_scope("product"):
        terms = pl.pallas_call(
            product_kernel,
            out_shape=jax.ShapeDtypeStruct((events, order.shape[0]), jnp.float32),
            in_specs=[vmem()] * (2 + len(parts)),
            out_specs=vmem(),
            compiler_params=params(),
            cost_estimate=cost(4 * events * order.shape[0] * span, 2 * order.shape[0] * span),
        )(impact, order[None], *parts)
    with jax.named_scope("sums"):
        shares = lax.all_to_all(terms[:, None, :], "asset", 0, 0)
        return jnp.sum(shares, axis=0)


def solution(mesh):
    in_specs = (
        P("ev", "asset"),
        P("asset", None),
        P(None, "asset"),
        P(None, "asset"),
        P(None, "asset"),
        P("asset"),
        P(),
        P(None, "asset"),
        P("ev"),
        P("ev", "asset"),
    )
    out_specs = P(("ev", "asset"), None)
    return jax.shard_map(shards, mesh=mesh, in_specs=in_specs, out_specs=out_specs, check_vma=False)
```
